32 devices in a mesh: dp: 8 (over z, core), tensor: 4 (over y, x).
Axes of the slice: x: 2, y: 2, z: 4, core: 2. Of those that a mesh axis runs over, the one named last changes fastest.
Arguments:
- token_ids: int32 [256], P('dp'), may hold values from 0 to 128255, as said below
- hidden_in: bfloat16 [256, 8192], P('dp'), may hold values from -6 to 6
- cotangent: bfloat16 [256, 8192], P('dp'), may hold values from -6 to 6
- gate_weight: bfloat16 [8192, 28672], P(None, ('dp', 'tensor')), may hold values from -0.0625 to 0.0625
- up_weight: bfloat16 [8192, 28672], P(None, ('dp', 'tensor')), may hold values from -0.0625 to 0.0625
- down_weight: bfloat16 [28672, 8192], P(('dp', 'tensor')), may hold values from -0.03125 to 0.03125
- gate_in_proj: bfloat16 [8192, 64], replicated, may hold values from -0.0625 to 0.0625
- up_in_proj: bfloat16 [8192, 64], replicated, may hold values from -0.0625 to 0.0625
- down_out_proj: bfloat16 [8192, 64], replicated, may hold values from -0.0625 to 0.0625
- gate_out_proj: bfloat16 [28672, 64], P(('dp', 'tensor')), may hold values from -0.03125 to 0.03125
- up_out_proj: bfloat16 [28672, 64], P(('dp', 'tensor')), may hold values from -0.03125 to 0.03125
- down_in_proj: bfloat16 [28672, 64], P(('dp', 'tensor')), may hold values from -0.03125 to 0.03125
- stored_grads: bfloat16 [1024, 12288], P(('dp', 'tensor')), may hold values from -0.0546875 to 0.0546875
- example_ids: int32 [1024], P(('dp', 'tensor')), may hold values from 0 to 255
Outputs:
- doc_grads: bfloat16 [8, 12288], P('dp')
- example_scores: float32 [8, 256], P(None, ('dp', 'tensor'))
The draws below stay inside these ranges and needn't reach their ends.
Inputs may be any that keep to these rules, and one draw needn't show every extreme that they name: `token_ids`: 0 marks padding, which only fills the end of a document of 32 tokens; each document has 16 or more tokens other than 0.
All inputs are finite; a program needn't handle non-finite values.
Results may differ from the reference program's by a relative error of at most 0.0051.
Values may be sent and summed in bfloat16 or wider, within the bound.
A program may use at most 128 MiB of HBM per device.

```python
import jax
import jax.numpy as jnp
from jax import lax

D = 8192
FF = 28672
VOCAB = 128256
R = 64
LEN = 32
DOCS = 8
TOKENS = 256
STORED = 1024
EXAMPLES = 256


def draw_token_ids(key, part):
    len_key = jax.random.fold_in(key, 11)
    tok_key = jax.random.fold_in(key, 12)
    kept_len = jax.random.randint(len_key, (DOCS, 1), LEN // 2, LEN + 1)
    word_ids = jax.random.randint(tok_key, (DOCS, LEN), 1, VOCAB)
    places = jnp.arange(LEN, dtype=jnp.int32)[None, :]
    return jnp.where(places < kept_len, word_ids, 0).reshape(DOCS * LEN).astype(jnp.int32)


def place_ends(values, own_key, least, largest):
    extent = values.shape
    place = [jax.random.randint(jax.random.fold_in(own_key, axis), (), 0, extent[axis]) for axis in range(len(extent))]
    values = values.at[tuple(place)].set(least)
    longest = extent.index(max(extent))
    place[longest] = (place[longest] + 1) % extent[longest]
    return values.at[tuple(place)].set(largest)


def shard_levels(own_key, shape, split, low, top_value):
    level, own = 1.0, jax.random.fold_in(own_key, 6)
    for axis_at, shards_of in split:
        heights = jnp.exp(jax.random.uniform(jax.random.fold_in(own, axis_at), (shards_of,), jnp.float32, low / len(split), top_value / len(split)))
        level = level * jnp.repeat(heights, shape[axis_at] // shards_of).reshape([-1 if axis == axis_at else 1 for axis in range(len(shape))])
    return level


def centred(rng, extent, scale, most, split=(), kind=jnp.bfloat16):
    entries = scale * jax.random.normal(rng, extent, jnp.float32)
    if split:
        entries = entries * shard_levels(rng, extent, split, -0.22, 0.18)
    return jnp.clip(entries, -most, most).astype(kind)


def setup_inputs(seed: int = 0) -> dict:
    streams_of = jax.random.split(jax.random.key(seed), 15)
    return {
        "token_ids": draw_token_ids(jax.random.fold_in(streams_of[14], 71), 0),
        "hidden_in": centred(streams_of[1], (TOKENS, D), 1.0, 6.0, ((0, 8),)),
        "cotangent": centred(streams_of[2], (TOKENS, D), 1.0, 6.0, ((0, 8),)),
        "gate_weight": centred(streams_of[3], (D, FF), D ** -0.5, 0.0625, ((1, 32),)),
        "up_weight": centred(streams_of[4], (D, FF), D ** -0.5, 0.0625, ((1, 32),)),
        "down_weight": centred(streams_of[5], (FF, D), FF ** -0.5, 0.03125, ((0, 32),)),
        "gate_in_proj": centred(streams_of[6], (D, R), D ** -0.5, 0.0625),
        "up_in_proj": centred(streams_of[7], (D, R), D ** -0.5, 0.0625),
        "down_out_proj": centred(streams_of[8], (D, R), D ** -0.5, 0.0625),
        "gate_out_proj": centred(streams_of[9], (FF, R), FF ** -0.5, 0.03125, ((0, 32),)),
        "up_out_proj": centred(streams_of[10], (FF, R), FF ** -0.5, 0.03125, ((0, 32),)),
        "down_in_proj": centred(streams_of[11], (FF, R), FF ** -0.5, 0.03125, ((0, 32),)),
        "stored_grads": centred(streams_of[12], (STORED, 3 * R * R), (3 * R * R) ** -0.5, 0.0546875, ((0, 32),)),
        "example_ids": place_ends(jax.random.randint(streams_of[13], (STORED,), 0, EXAMPLES), jax.random.fold_in(streams_of[13], 1), 0, EXAMPLES - 1).astype(jnp.int32),
    }


def doc_outer(left, right):
    left_docs = left.reshape(DOCS, LEN, R)
    right_docs = right.reshape(DOCS, LEN, R)
    return jnp.einsum("dlr,dls->drs", left_docs, right_docs, precision=lax.Precision.HIGHEST)


def reference(token_ids, hidden_in, cotangent, gate_weight, up_weight, down_weight, gate_in_proj, up_in_proj, down_out_proj, gate_out_proj, up_out_proj, down_in_proj, stored_grads, example_ids):
    pad_mask = (token_ids != 0).astype(jnp.bfloat16)[:, None]
    masked = cotangent * pad_mask
    gate_pre = jnp.dot(hidden_in, gate_weight, preferred_element_type=jnp.float32)
    up_pre = jnp.dot(hidden_in, up_weight, preferred_element_type=jnp.float32)
    squash = jax.nn.sigmoid(gate_pre)
    hidden = (gate_pre * squash * up_pre).astype(jnp.bfloat16)
    back_pre = lax.dot_general(masked, down_weight, (((1,), (1,)), ((), ())), preferred_element_type=jnp.float32)
    grad_up = (back_pre * gate_pre * squash).astype(jnp.bfloat16)
    grad_gate = (back_pre * up_pre * squash * (1.0 + gate_pre * (1.0 - squash))).astype(jnp.bfloat16)
    side_gate = jnp.dot(grad_gate, gate_out_proj, preferred_element_type=jnp.float32)
    side_up = jnp.dot(grad_up, up_out_proj, preferred_element_type=jnp.float32)
    side_down = jnp.dot(hidden, down_in_proj, preferred_element_type=jnp.float32)
    in_gate = jnp.dot(hidden_in, gate_in_proj, preferred_element_type=jnp.float32)
    in_up = jnp.dot(hidden_in, up_in_proj, preferred_element_type=jnp.float32)
    out_down = jnp.dot(masked, down_out_proj, preferred_element_type=jnp.float32)
    blocks = jnp.stack([doc_outer(in_gate, side_gate), doc_outer(in_up, side_up), doc_outer(side_down, out_down)], axis=1)
    doc_grads = blocks.reshape(DOCS, 3 * R * R).astype(jnp.bfloat16)
    scores = lax.dot_general(doc_grads, stored_grads, (((1,), (1,)), ((), ())), preferred_element_type=jnp.float32)
    onehot = (example_ids[:, None] == jnp.arange(EXAMPLES, dtype=jnp.int32)[None, :]).astype(jnp.float32)
    example_scores = jnp.dot(scores, onehot, precision=lax.Precision.HIGHEST)
    return doc_grads, example_scores
```

```python
import functools

import jax
import jax.numpy as jnp
from jax import lax
from jax.experimental import pallas as pl
from jax.experimental.pallas import tpu as pltpu
from jax.sharding import PartitionSpec as P

EX_DEV = 8
CORES = 2
SUBS = 2
F32 = jnp.float32
BF16 = jnp.bfloat16
HIGH = lax.Precision.HIGHEST


def await_bytes(ref, sem):
    pltpu.make_async_copy(ref, ref, sem).wait()


def kernel(
    dp,
    tp,
    tok_ref,
    ids_ref,
    hid_ref,
    cot_ref,
    gate_ref,
    up_ref,
    down_ref,
    gin_ref,
    uin_ref,
    dout_ref,
    gout_ref,
    uout_ref,
    din_ref,
    stored_ref,
    grads_out,
    scores_out,
    acts,
    cot_tmp,
    w_buf,
    d_buf,
    in_buf,
    out_buf,
    stored_buf,
    acc,
    in_acc,
    sides,
    side_tx,
    side_rx,
    part_tx,
    part_rx,
    g_sq,
    g_all,
    g_f32,
    g_rows,
    ex_tx,
    ex_rx,
    load_sem,
    w_sem,
    d_sem,
    z_send,
    z_recv,
    p_send,
    p_recv,
    c_send,
    c_recv,
    t_send,
    t_recv,
):
    outer = dp // CORES
    devices = dp * tp
    rows = hid_ref.shape[0]
    width = acts.shape[-1]
    rank = gin_ref.shape[1]
    phases = 2 * SUBS
    d = lax.axis_index("dp")
    t = lax.axis_index("tensor")
    o = d // CORES
    c = d % CORES
    me = d * tp + t
    own = c * outer + o

    def send(src, dst, send_sem, recv_sem, to_d, to_t):
        pltpu.make_async_remote_copy(
            src_ref=src,
            dst_ref=dst,
            send_sem=send_sem,
            recv_sem=recv_sem,
            device_id=(to_d, to_t),
            device_id_type=pl.DeviceIdType.MESH,
        ).start()

    def cols(sub, part):
        return pl.ds(pl.multiple_of((sub * tp + part) * width, width), width)

    cot_load = pltpu.make_async_copy(cot_ref, cot_tmp, load_sem.at[0])
    cot_load.start()
    for sub in range(SUBS):
        for part in range(tp):
            pltpu.make_async_copy(
                hid_ref.at[:, cols(sub, part)], acts.at[sub, part, c, o], load_sem.at[1]
            ).start()

    def weight_loads(sub, part):
        return [
            pltpu.make_async_copy(
                ref.at[cols(sub, part), :], w_buf.at[k, part], w_sem.at[k, part]
            )
            for k, ref in enumerate((gate_ref, up_ref))
        ]

    def down_load(sub, part):
        return pltpu.make_async_copy(
            down_ref.at[:, cols(sub, part)], d_buf.at[sub * tp + part], d_sem.at[sub * tp + part]
        )

    barrier = pltpu.get_barrier_semaphore()

    def greet(k, carry):
        other = (me + k) % devices
        pl.semaphore_signal(
            barrier,
            inc=1,
            device_id=(other // tp, other % tp),
            device_id_type=pl.DeviceIdType.MESH,
        )
        return carry

    lax.fori_loop(1, devices, greet, 0)
    pl.semaphore_wait(barrier, devices - 1)

    def z_sends(p, src):
        for k in range(1, outer):
            to_o = (o + k) % outer
            send(
                src,
                acts.at[p, t, c, o],
                z_send.at[p],
                z_recv.at[p, k],
                to_o * CORES + c,
                t,
            )

    for sub in range(SUBS):
        z_sends(sub, hid_ref.at[:, cols(sub, t)])

    for part in range(tp):
        for load in weight_loads(0, part):
            load.start()
    in_loads = [
        pltpu.make_async_copy(ref, in_buf.at[k], load_sem.at[2 + k])
        for k, ref in enumerate((gin_ref, uin_ref, dout_ref))
    ]
    out_loads = [
        pltpu.make_async_copy(ref, out_buf.at[k], load_sem.at[5 + k])
        for k, ref in enumerate((gout_ref, uout_ref, din_ref))
    ]
    stored_load = pltpu.make_async_copy(stored_ref, stored_buf, load_sem.at[8])
    for load in in_loads:
        load.start()

    cot_load.wait()
    lane = lax.broadcasted_iota(jnp.int32, (rows, rows), 1)
    line = lax.broadcasted_iota(jnp.int32, (rows, rows), 0)
    kept = (tok_ref[...] != 0).astype(F32)
    mask = jnp.sum(jnp.where(lane == line, kept, 0.0), axis=1, keepdims=True)
    for sub in range(SUBS):
        for part in range(tp):
            piece = cot_tmp[:, (sub * tp + part) * width : (sub * tp + part + 1) * width]
            acts[SUBS + sub, part, c, o] = (piece.astype(F32) * mask).astype(BF16)
    for sub in range(SUBS):
        z_sends(SUBS + sub, acts.at[SUBS + sub, t, c, o])
    await_bytes(acts.at[0:SUBS, :, 0, 0], load_sem.at[1])
    for sub in range(SUBS):
        for part in range(tp):
            down_load(sub, part).start()
    for load in out_loads:
        load.start()
    stored_load.start()
    acc[...] = jnp.zeros_like(acc)
    in_acc[...] = jnp.zeros_like(in_acc)

    relay = tp == 4
    if relay:
        x_nb = t + 1 - 2 * (t % 2)
        y_nb = (t + 2) % 4
        first = x_nb + c * (y_nb - x_nb)
        second = y_nb + c * (x_nb - y_nb)
        direct = [first, second]
        diagonal = 3 - t
        others = [first, second, diagonal]
    else:
        direct = [(t + k) % tp for k in range(1, tp)]
        others = [(t + tp - k) % tp for k in range(1, tp)]

    def to_core(p, part):
        send(
            acts.at[p, part, c],
            acts.at[p, part, c],
            c_send.at[p],
            c_recv.at[p],
            o * CORES + 1 - c,
            t,
        )

    def spread(p):
        for k in range(1, outer):
            piece = acts.at[p, t, c, (o + outer - k) % outer]
            await_bytes(piece, z_recv.at[p, k])
            for to_t in direct:
                send(piece, piece, p_send.at[p], p_recv.at[p, t, k], d, to_t)
        to_core(p, t)

    def collect(p):
        for at, part in enumerate(others):
            for k in range(1, outer):
                piece = acts.at[p, part, c, (o + outer - k) % outer]
                await_bytes(piece, p_recv.at[p, part, k])
                if relay and at == 0:
                    send(piece, piece, p_send.at[p], p_recv.at[p, part, k], d, second)
            to_core(p, part)
        await_bytes(acts.at[p, :, 0], c_recv.at[p])

    def forward_part(sub, part):
        for load in weight_loads(sub, part):
            load.wait()
        lhs = acts[sub, part].reshape(dp * rows, width)
        for k in range(2):
            acc[k] += jnp.dot(lhs, w_buf[k, part], preferred_element_type=F32)
            in_acc[k] += jnp.dot(lhs, in_buf[k, cols(sub, part), :], preferred_element_type=F32)
        if sub + 1 < SUBS:
            for load in weight_loads(sub + 1, part):
                load.start()

    def backward_part(sub, part):
        down_load(sub, part).wait()
        lhs = acts[SUBS + sub, part].reshape(dp * rows, width)
        acc[2] += lax.dot_general(
            lhs, d_buf[sub * tp + part], (((1,), (1,)), ((), ())), preferred_element_type=F32
        )
        in_acc[2] += jnp.dot(lhs, in_buf[2, cols(sub, part), :], preferred_element_type=F32)

    def each_part(body):
        def step(part, carry):
            body(part)
            return carry

        lax.fori_loop(0, tp, step, 0)

    def line_block(j):
        return pl.ds(pl.multiple_of(j * rows, rows), rows)

    def gates(j, carry):
        at = line_block(j)
        gate_pre = acc[0, at, :]
        up_pre = acc[1, at, :]
        squash = jax.nn.sigmoid(gate_pre)
        gated = gate_pre * squash
        sides[2, at, :] = (gated * up_pre).astype(BF16)
        acc[0, at, :] = gated
        acc[1, at, :] = up_pre * squash * (1.0 + gate_pre * (1.0 - squash))
        return carry

    def grads(j, carry):
        at = line_block(j)
        back = acc[2, at, :]
        sides[1, at, :] = (back * acc[0, at, :]).astype(BF16)
        sides[0, at, :] = (back * acc[1, at, :]).astype(BF16)
        return carry

    spread(0)
    for p in range(phases):
        if p + 1 < phases:
            spread(p + 1)
        collect(p)
        if p == 0:
            in_loads[0].wait()
            in_loads[1].wait()
        if p == SUBS:
            in_loads[2].wait()
        if p < SUBS:
            each_part(functools.partial(forward_part, p))
        else:
            each_part(functools.partial(backward_part, p - SUBS))
        if p == SUBS - 1:
            lax.fori_loop(0, dp, gates, 0)
            for load in out_loads:
                load.wait()
    lax.fori_loop(0, dp, grads, 0)

    for k in range(3):
        side = jnp.dot(sides[k], out_buf[k], preferred_element_type=F32)
        side_tx[k] = side.astype(BF16).reshape(dp, rows, rank)
        part_tx[k] = side_tx[k, own].astype(F32)

    for k in range(1, dp):
        to_d = (d + k) % dp
        row = (to_d % CORES) * outer + to_d // CORES
        send(
            side_tx.at[:, row], side_rx.at[k], t_send.at[0], t_recv.at[0], to_d, t
        )
    await_bytes(side_rx.at[1:dp], t_recv.at[0])
    for k in range(1, dp):
        part_tx[...] += side_rx[k].astype(F32)
    for k in range(1, tp):
        send(part_tx, part_rx.at[k], t_send.at[1], t_recv.at[1], d, (t + k) % tp)
    await_bytes(part_rx.at[1:tp], t_recv.at[1])
    part_rx[0] = part_tx[...]
    side_sum = jnp.zeros((3, rows, rank), F32)
    for s in range(tp):
        side_sum += part_rx[(t + tp - s) % tp]

    at = line_block(own)
    for k in range(3):
        left, right = in_acc[k, at, :], side_sum[k]
        if k == 2:
            left, right = right, left
        g_sq[k] = lax.dot_general(
            left, right, (((0,), (0,)), ((), ())), precision=HIGH, preferred_element_type=F32
        )
    half = rank // 2
    lines = 3 * half
    for k in range(3):
        even = g_sq[k, pl.ds(0, half, stride=2), :]
        odd = g_sq[k, pl.ds(1, half, stride=2), :]
        g_all[d, k * half : (k + 1) * half, :] = jnp.concatenate([even, odd], axis=1).astype(BF16)
    grads_out[...] = g_all[d]
    for k in range(1, dp):
        send(g_all.at[d], g_all.at[d], t_send.at[2], t_recv.at[2], (d + k) % dp, t)
    stored_load.wait()
    await_bytes(g_all.at[1:dp], t_recv.at[2])
    g_f32[...] = g_all[...].astype(F32)
    for i in range(lines):
        g_rows[:, i * 2 * rank : (i + 1) * 2 * rank] = g_f32[:, i, :]
    raw = lax.dot_general(
        g_rows[...].astype(BF16),
        stored_buf[...],
        (((1,), (1,)), ((), ())),
        preferred_element_type=F32,
    )
    stored_rows = stored_buf.shape[0]
    hot = (
        lax.broadcasted_iota(jnp.int32, (devices * EX_DEV, stored_rows), 0) == ids_ref[...]
    ).astype(F32)
    scattered = lax.dot_general(
        hot, raw, (((1,), (1,)), ((), ())), precision=HIGH, preferred_element_type=F32
    )
    ex_tx[...] = scattered.reshape(devices, EX_DEV, dp)

    def scatter(k, carry):
        other = (me + k) % devices
        send(
            ex_tx.at[other], ex_rx.at[k], t_send.at[3], t_recv.at[3], other // tp, other % tp
        )
        return carry

    lax.fori_loop(1, devices, scatter, 0)
    ex_rx[0] = ex_tx[me]
    await_bytes(ex_rx.at[1:devices], t_recv.at[3])
    scores_out[...] = jnp.sum(ex_rx[...], axis=0)

    for p in range(phases):
        await_bytes(acts.at[p, 0, 0, 1:outer], z_send.at[p])
        await_bytes(acts.at[p, 1:tp, 0, 1:outer], p_send.at[p])
        await_bytes(acts.at[p, :, 0], c_send.at[p])
    await_bytes(side_rx.at[1:dp], t_send.at[0])
    await_bytes(part_rx.at[1:tp], t_send.at[1])
    await_bytes(g_all.at[1:dp], t_send.at[2])
    await_bytes(ex_rx.at[1:devices], t_send.at[3])


def body(dp, tp, *args):
    (
        token_ids,
        hidden_in,
        cotangent,
        gate_weight,
        up_weight,
        down_weight,
        gate_in_proj,
        up_in_proj,
        down_out_proj,
        gate_out_proj,
        up_out_proj,
        down_in_proj,
        stored_grads,
        example_ids,
    ) = args
    rows, model = hidden_in.shape
    hidden_here = gate_weight.shape[1]
    rank = gate_in_proj.shape[1]
    outer = dp // CORES
    devices = dp * tp
    width = model // (tp * SUBS)
    phases = 2 * SUBS
    lines = 3 * rank // 2
    tokens = dp * rows
    dma = pltpu.SemaphoreType.DMA
    vmem = pl.BlockSpec(memory_space=pltpu.VMEM)
    hbm = pl.BlockSpec(memory_space=pl.ANY)
    doc_lines, scores = pl.pallas_call(
        functools.partial(kernel, dp, tp),
        out_shape=(
            jax.ShapeDtypeStruct((lines, 2 * rank), BF16),
            jax.ShapeDtypeStruct((EX_DEV, dp), F32),
        ),
        in_specs=[vmem] * 2 + [hbm] * 12,
        out_specs=(vmem, vmem),
        scratch_shapes=[
            pltpu.VMEM((phases, tp, CORES, outer, rows, width), BF16),
            pltpu.VMEM((rows, model), BF16),
            pltpu.VMEM((2, tp, width, hidden_here), BF16),
            pltpu.VMEM((SUBS * tp, hidden_here, width), BF16),
            pltpu.VMEM((3, model, rank), BF16),
            pltpu.VMEM((3, hidden_here, rank), BF16),
            pltpu.VMEM(stored_grads.shape, BF16),
            pltpu.VMEM((3, tokens, hidden_here), F32),
            pltpu.VMEM((3, tokens, rank), F32),
            pltpu.VMEM((3, tokens, hidden_here), BF16),
            pltpu.VMEM((3, dp, rows, rank), BF16),
            pltpu.VMEM((dp, 3, rows, rank), BF16),
            pltpu.VMEM((3, rows, rank), F32),
            pltpu.VMEM((tp, 3, rows, rank), F32),
            pltpu.VMEM((3, rank, rank), F32),
            pltpu.VMEM((dp, lines, 2 * rank), BF16),
            pltpu.VMEM((dp, lines, 2 * rank), F32),
            pltpu.VMEM((dp, lines * 2 * rank), F32),
            pltpu.VMEM((devices, EX_DEV, dp), F32),
            pltpu.VMEM((devices, EX_DEV, dp), F32),
            dma((9,)),
            dma((2, tp)),
            dma((SUBS * tp,)),
            dma((phases,)),
            dma((phases, outer)),
            dma((phases,)),
            dma((phases, tp, outer)),
            dma((phases,)),
            dma((phases,)),
            dma((4,)),
            dma((4,)),
        ],
        compiler_params=pltpu.CompilerParams(
            collective_id=0, has_side_effects=True, vmem_limit_bytes=60 * 2**20
        ),
    )(
        token_ids.reshape(1, rows),
        example_ids.reshape(1, -1),
        hidden_in,
        cotangent,
        gate_weight,
        up_weight,
        down_weight,
        gate_in_proj,
        up_in_proj,
        down_out_proj,
        gate_out_proj,
        up_out_proj,
        down_in_proj,
        stored_grads,
    )
    return doc_lines.reshape(1, lines * 2 * rank), scores.T


def solution(mesh):
    return jax.shard_map(
        functools.partial(body, mesh.shape["dp"], mesh.shape["tensor"]),
        mesh=mesh,
        in_specs=(
            P("dp"),
            P("dp", None),
            P("dp", None),
            P(None, ("dp", "tensor")),
            P(None, ("dp", "tensor")),
            P(("dp", "tensor"), None),
            P(),
            P(),
            P(),
            P(("dp", "tensor"), None),
            P(("dp", "tensor"), None),
            P(("dp", "tensor"), None),
            P(("dp", "tensor"), None),
            P(("dp", "tensor")),
        ),
        out_specs=(P("dp", None), P(None, ("dp", "tensor"))),
        check_vma=False,
    )
```
